256 devices in a mesh: frame: 8 (over z_lo, core), row: 32 (over y, x, z_hi).
Axes of the slice: x: 4, y: 4, z: 8 (z_hi: 2, z_lo: 4; z = z_hi * 4 + z_lo), core: 2. Of those that a mesh axis runs over, the one named last changes fastest.
Arguments:
- latent: bfloat16 [32, 32, 40, 1152], P('frame', 'row'), may hold values from -6 to 6
- mod_spatial: float32 [3, 1152], replicated, may hold values from -3 to 3
- mod_temporal: float32 [3, 1152], replicated, may hold values from -3 to 3
- qk_gain: float32 [4, 72], replicated, may hold values from 0.7 to 6, as said below
- w_qkv_spatial: bfloat16 [1152, 3456], P('row'), may hold values from -0.1875 to 0.1875
- w_out_spatial: bfloat16 [1152, 1152], P('row'), may hold values from -0.1875 to 0.1875
- w_qkv_temporal: bfloat16 [1152, 3456], P('row'), may hold values from -0.1875 to 0.1875
- w_out_temporal: bfloat16 [1152, 1152], P('row'), may hold values from -0.1875 to 0.1875
Outputs:
- mixed: bfloat16 [32, 32, 40, 1152], P('frame', 'row')
The draws below stay inside these ranges and needn't reach their ends.
Inputs may be any that keep to these rules, and one draw needn't show every extreme that they name: `qk_gain`: gains of the per-head query and key norms.
All inputs are finite; a program needn't handle non-finite values.
Results may differ from the reference program's by a relative error of at most 0.028.
Values may be sent and summed in bfloat16 or wider, within the bound.
No kernel may reach another device: no remote copies, remote signals or barrier semaphores. Data moves between devices by JAX's collectives and lax.ppermute only.
A program may use at most 128 MiB of HBM per device.

```python
import jax
import jax.numpy as jnp
from jax import lax

D = 1152
HEADS = 16
HDIM = 72
WP = 40
FRAMES = 32
HP = 32


def draw_qk_gain(key, part):
    key = jax.random.fold_in(key, 11)
    return 1.0 + jax.random.uniform(key, (4, HDIM), jnp.float32, -0.3, 0.3)


def block_levels(stream_key, extent, split, least, top_value):
    def one(dim, shards_of):
        draws = jax.random.uniform(jax.random.fold_in(jax.random.fold_in(stream_key, 6), dim), (shards_of,), jnp.float32, least / len(split), top_value / len(split))
        return jnp.repeat(jnp.exp(draws), extent[dim] // shards_of).reshape((-1,) + (1,) * (len(extent) - dim - 1))

    loudness = one(*split[0])
    for cut in split[1:]:
        loudness = loudness * one(*cut)
    return loudness


def bell_draw(stream_key, extent, spread, bound, split=(), kind=jnp.bfloat16):
    loudness = block_levels(stream_key, extent, split, -0.22, 0.18) if split else 1.0
    array = jax.random.normal(stream_key, extent, jnp.float32) * spread * loudness
    return jnp.minimum(jnp.maximum(array, -bound), bound).astype(kind)


def setup_inputs(seed: int = 0) -> dict:
    seeds = jax.random.split(jax.random.key(seed), 9)
    latent = bell_draw(seeds[0], (FRAMES, HP, WP, D), 1.0, 6.0, ((0, 8), (1, 32)))
    mod_spatial = bell_draw(seeds[1], (3, D), 0.5, 3.0, (), jnp.float32)
    mod_temporal = bell_draw(seeds[2], (3, D), 0.5, 3.0, (), jnp.float32)
    qk_gain = draw_qk_gain(jax.random.fold_in(seeds[8], 71), 0)
    w_qkv_spatial = bell_draw(seeds[4], (D, 3 * D), D ** -0.5, 0.1875, ((0, 32),))
    w_out_spatial = bell_draw(seeds[5], (D, D), D ** -0.5, 0.1875, ((0, 32),))
    w_qkv_temporal = bell_draw(seeds[6], (D, 3 * D), D ** -0.5, 0.1875, ((0, 32),))
    w_out_temporal = bell_draw(seeds[7], (D, D), D ** -0.5, 0.1875, ((0, 32),))
    return {"latent": latent, "mod_spatial": mod_spatial, "mod_temporal": mod_temporal, "qk_gain": qk_gain, "w_qkv_spatial": w_qkv_spatial, "w_out_spatial": w_out_spatial, "w_qkv_temporal": w_qkv_temporal, "w_out_temporal": w_out_temporal}


def modulate(tokens_in, modulation):
    values = tokens_in.astype(jnp.float32)
    center = values - lax.optimization_barrier(jnp.mean(values, -1, keepdims=True))
    variance = lax.optimization_barrier(jnp.mean(center * center, -1, keepdims=True))
    normed = center * lax.rsqrt(variance + 1e-06)
    return (normed * (1.0 + modulation[1]) + modulation[0]).astype(jnp.bfloat16)

def head_norm(heads_in, gain):
    square = lax.optimization_barrier(jnp.mean(heads_in * heads_in, -1, keepdims=True))
    return (heads_in * lax.rsqrt(square + 1e-06) * gain).astype(jnp.bfloat16)

def make_heads(modulated, weight, gain_query, gain_key):
    lead = modulated.shape[:-1]
    qkv = jnp.dot(modulated.reshape(-1, D), weight, preferred_element_type=jnp.float32)
    qkv = qkv.reshape(lead + (3, HEADS, HDIM))
    queries = head_norm(qkv[..., 0, :, :], gain_query)
    keyset = head_norm(qkv[..., 1, :, :], gain_key)
    values = qkv[..., 2, :, :].astype(jnp.bfloat16)
    return (queries, keyset, values)

def add_branch(tokens_in, attended, weight, modulation):
    projected = jnp.dot(attended.reshape(-1, D), weight, preferred_element_type=jnp.float32)
    projected = projected.reshape(tokens_in.shape)
    return (tokens_in.astype(jnp.float32) + modulation[2] * projected).astype(jnp.bfloat16)

def frame_attend(items):
    queries, keyset, values = items
    scores = jnp.einsum('qhd,khd->hqk', queries.astype(jnp.float32), keyset.astype(jnp.float32)) / jnp.sqrt(jnp.float32(HDIM))
    highest = lax.optimization_barrier(jnp.max(scores, -1, keepdims=True))
    expo = jnp.exp(scores - highest)
    probabilities = (expo / lax.optimization_barrier(jnp.sum(expo, -1, keepdims=True))).astype(jnp.bfloat16)
    return jnp.einsum('hqk,khd->qhd', probabilities.astype(jnp.float32), values.astype(jnp.float32)).astype(jnp.bfloat16)

def reference(latent, mod_spatial, mod_temporal, qk_gain, w_qkv_spatial, w_out_spatial, w_qkv_temporal, w_out_temporal):
    frame_tokens = HP * WP
    modulated = modulate(latent, mod_spatial)
    queries, keyset, values = make_heads(modulated, w_qkv_spatial, qk_gain[0], qk_gain[1])
    shape_frame = (FRAMES, frame_tokens, HEADS, HDIM)
    attended = lax.map(frame_attend, (queries.reshape(shape_frame), keyset.reshape(shape_frame), values.reshape(shape_frame)))
    hidden = add_branch(latent, attended, w_out_spatial, mod_spatial)
    modulated = modulate(hidden, mod_temporal)
    queries, keyset, values = make_heads(modulated, w_qkv_temporal, qk_gain[2], qk_gain[3])
    queries = queries.reshape(shape_frame).astype(jnp.float32)
    keyset = keyset.reshape(shape_frame).astype(jnp.float32)
    values = values.reshape(shape_frame).astype(jnp.float32)
    scores = jnp.einsum('fthd,gthd->thfg', queries, keyset) / jnp.sqrt(jnp.float32(HDIM))
    highest = lax.optimization_barrier(jnp.max(scores, -1, keepdims=True))
    expo = jnp.exp(scores - highest)
    probabilities = (expo / lax.optimization_barrier(jnp.sum(expo, -1, keepdims=True))).astype(jnp.bfloat16)
    attended = jnp.einsum('thfg,gthd->fthd', probabilities.astype(jnp.float32), values).astype(jnp.bfloat16)
    return add_branch(hidden, attended, w_out_temporal, mod_temporal)
```

```python
import jax
import jax.numpy as jnp
from jax import lax
from jax.sharding import Mesh
from jax.sharding import PartitionSpec as P

HEADS = 16
HDIM = 72
D = 1152


def modulate(tokens_in, modulation):
    values = tokens_in.astype(jnp.float32)
    center = values - jnp.mean(values, -1, keepdims=True)
    variance = jnp.mean(center * center, -1, keepdims=True)
    normed = center * lax.rsqrt(variance + 1e-06)
    return (normed * (1.0 + modulation[1]) + modulation[0]).astype(jnp.bfloat16)


def head_norm(heads_in, gain):
    square = jnp.mean(heads_in * heads_in, -1, keepdims=True)
    return (heads_in * lax.rsqrt(square + 1e-06) * gain).astype(jnp.bfloat16)


def softmax(scores):
    highest = jnp.max(scores, -1, keepdims=True)
    expo = jnp.exp(scores - highest)
    return (expo / jnp.sum(expo, -1, keepdims=True)).astype(jnp.bfloat16)


def dot32(a, b):
    return jnp.dot(a, b, preferred_element_type=jnp.float32)


def spatial_attend(tokens, weight, gain_q, gain_k):
    qkv = dot32(tokens, weight).reshape(tokens.shape[0], 3, 2, HDIM)
    scale = 1.0 / jnp.sqrt(jnp.float32(HDIM))
    outs = []
    for head in range(2):
        q = head_norm(qkv[:, 0, head], gain_q)
        k = head_norm(qkv[:, 1, head], gain_k)
        v = qkv[:, 2, head].astype(jnp.bfloat16)
        probs = softmax(jnp.einsum("qd,kd->qk", q, k, preferred_element_type=jnp.float32) * scale)
        outs.append(dot32(probs, v).astype(jnp.bfloat16))
    return jnp.concatenate(outs, -1)


def temporal_attend(qkv, gain_q, gain_k):
    q = head_norm(qkv[:, :, 0], gain_q)
    k = head_norm(qkv[:, :, 1], gain_k)
    v = qkv[:, :, 2].astype(jnp.bfloat16)
    scale = 1.0 / jnp.sqrt(jnp.float32(HDIM))
    scores = jnp.einsum("fphd,gphd->phfg", q, k, preferred_element_type=jnp.float32) * scale
    probs = softmax(scores)
    return jnp.einsum("phfg,gphd->fphd", probs, v, preferred_element_type=jnp.float32).astype(
        jnp.bfloat16
    )


def per_device(latent, mod_s, mod_t, gain, wqkv_s, wout_s, wqkv_t, wout_t):
    core = lax.axis_index("core")
    zh = lax.axis_index("zh")
    by_pair = wqkv_s.reshape(36, 3, 4, 2, 2 * HDIM)
    half_s = lax.dynamic_index_in_dim(by_pair, core, 3, keepdims=False)
    half_s = half_s.transpose(0, 2, 1, 3).reshape(36, 4 * 432)
    rest = jnp.concatenate([wout_s, wqkv_t, wout_t, jnp.zeros((36, 128), jnp.bfloat16)], 1)
    half_r = lax.dynamic_slice_in_dim(rest, core * 2944, 2944, 1)

    modulated = modulate(latent, mod_s).reshape(4, 40, D)
    y = lax.axis_index("y")
    swap = [(c * 2 + z, z * 2 + c) for c in range(2) for z in range(2)]
    swapped = lax.ppermute(modulated, ("core", "zh"), swap)
    frame_rows = lax.all_to_all(swapped, "y", split_axis=0, concat_axis=0, tiled=True)

    mine = jnp.concatenate([half_s, half_r], 1)
    other = lax.ppermute(mine, "zh", [(0, 1), (1, 0)])
    low = jnp.where(zh == 0, mine, other)
    high = jnp.where(zh == 0, other, mine)
    both = jnp.concatenate([low, high], 0)
    both_s = both[:, :1728].reshape(72, 4, 432).transpose(1, 0, 2)
    both_s = jnp.broadcast_to(both_s[None], (4, 4, 72, 432)).reshape(16, 72, 432)
    w_s = lax.all_to_all(both_s, ("y", "x"), split_axis=0, concat_axis=0, tiled=True)
    w_s = w_s.reshape(D, 432)

    gathered = lax.all_gather(both[:, 1728:], ("y", "x"), axis=0, tiled=True)
    pair = lax.ppermute(gathered, "core", [(0, 1), (1, 0)])
    w0 = jnp.where(core == 0, gathered, pair)
    w1 = jnp.where(core == 0, pair, gathered)
    wo_s = w0[:, :D]

    frame_rows = frame_rows.reshape(160, D)
    in_x = lax.all_to_all(
        jnp.broadcast_to(frame_rows[None], (4, 160, D)), "x", split_axis=0, concat_axis=0, tiled=True
    )
    in_core = lax.ppermute(in_x, "core", [(0, 1), (1, 0)])
    tok = jnp.concatenate([in_x, in_core], 0).reshape(1280, D)

    attended = spatial_attend(tok, w_s, gain[0], gain[1])
    att = attended.reshape(2, 4, 4, 4, 2, 5, 2 * HDIM)
    att = jnp.where(core == 0, att, att[::-1])
    att = att.transpose(3, 0, 2, 1, 4, 5, 6).reshape(256, 5, 2 * HDIM)
    everyone = ("zl", "zh", "y", "x", "core")
    back = lax.all_to_all(att, everyone, split_axis=0, concat_axis=0, tiled=True)
    back = back.reshape(32, 8, 5, 2 * HDIM).transpose(0, 2, 1, 3).reshape(160, D)

    home = lax.all_to_all(
        latent.reshape(4, 40, D), ("zl", "core"), split_axis=1, concat_axis=0, tiled=True
    )
    residual = home.reshape(160, D).astype(jnp.float32)
    hidden = (residual + mod_s[2] * dot32(back, wo_s)).astype(jnp.bfloat16)

    modulated = modulate(hidden, mod_t)
    qkv = jnp.concatenate(
        [dot32(modulated, w0[:, D:]), dot32(modulated, w1[:, : 3 * D - 1792])], 1
    ).reshape(32, 5, 3, HEADS, HDIM)
    att_t = temporal_attend(qkv, gain[2], gain[3]).reshape(160, D)
    wo_t = w1[:, 3 * D - 1792 : 4 * D - 1792]
    mixed = (hidden.astype(jnp.float32) + mod_t[2] * dot32(att_t, wo_t)).astype(jnp.bfloat16)
    mixed = lax.all_to_all(
        mixed.reshape(32, 5, D), ("zl", "core"), split_axis=0, concat_axis=1, tiled=True
    )
    return mixed.reshape(4, 1, 40, D)


def solution(mesh):
    fine = Mesh(mesh.devices.reshape(4, 2, 4, 4, 2), ("zl", "core", "y", "x", "zh"))
    frame, row = ("zl", "core"), ("y", "x", "zh")
    in_specs = (
        P(frame, row, None, None),
        P(),
        P(),
        P(),
        P(row, None),
        P(row, None),
        P(row, None),
        P(row, None),
    )
    return jax.shard_map(
        per_device,
        mesh=fine,
        in_specs=in_specs,
        out_specs=P(frame, row, None, None),
        check_vma=False,
    )
```

```python
import jax
import jax.numpy as jnp
from jax import lax
from jax.experimental import pallas as pl
from jax.experimental.pallas import tpu as pltpu
from jax.sharding import Mesh
from jax.sharding import PartitionSpec as P

HEADS = 16
HDIM = 72
D = 1152
PAIR = 2 * HDIM
CUT = 2944
REST = 3 * D - CUT
SCALE = HDIM**-0.5
EXP2 = 1.4426950408889634
F32 = jnp.float32
BF16 = jnp.bfloat16
VMEM = pl.BlockSpec(memory_space=pltpu.VMEM)
SMEM = pl.BlockSpec(memory_space=pltpu.SMEM)
ANY = pl.BlockSpec(memory_space=pl.ANY)


def dot32(a, b):
    return jnp.dot(a, b, preferred_element_type=F32)


def dot_t(a, b):
    return lax.dot_general(a, b, (((1,), (1,)), ((), ())), preferred_element_type=F32)


def modulate(values, shift, scale):
    center = values - jnp.mean(values, -1, keepdims=True)
    variance = jnp.mean(center * center, -1, keepdims=True)
    return (center * lax.rsqrt(variance + 1e-06) * (1.0 + scale) + shift).astype(BF16)


def merge_kernel(place, mod, a0, a1, a2, a3, out):
    for k, piece in enumerate((a0, a1, a2, a3)):
        rows = modulate(piece[...].astype(F32), mod[0:1], mod[1:2])
        for copy in range(4):
            out[copy, lax.rem(place[0] + k, 4)] = rows


def merge(place, mod, pieces):
    return pl.pallas_call(
        merge_kernel,
        out_shape=jax.ShapeDtypeStruct((4, 4, 40, D), BF16),
        in_specs=[SMEM] + [VMEM] * 5,
        out_specs=VMEM,
        cost_estimate=pl.CostEstimate(
            flops=4_000_000, bytes_accessed=2_000_000, transcendentals=0
        ),
    )(place, mod, *pieces)


def softmax(scores):
    highest = jnp.max(scores, -1, keepdims=True)
    expo = jnp.exp2((scores - highest) * (SCALE * EXP2))
    return (expo * (1.0 / jnp.sum(expo, -1, keepdims=True))).astype(BF16)


def spatial_kernel(place, gain, tok_ours, tok_theirs, wts, out, wall, q0, q1, k0, v0):
    core = place[1]
    wall[...] = jnp.zeros_like(wall)
    for part in range(3):
        wall[:, 256 * part : 256 * part + PAIR] = wts[:, PAIR * part : PAIR * (part + 1)]
    lane = lax.broadcasted_iota(jnp.int32, (1, 256), 1)
    first = lane < HDIM
    second = (lane >= HDIM) & (lane < PAIR)

    def head_norm(heads, g):
        square = heads * heads
        s0 = jnp.sum(jnp.where(first, square, 0.0), -1, keepdims=True)
        s1 = jnp.sum(jnp.where(first, 0.0, square), -1, keepdims=True)
        r0 = lax.rsqrt(s0 * (1.0 / HDIM) + 1e-06)
        r1 = lax.rsqrt(s1 * (1.0 / HDIM) + 1e-06)
        return heads * jnp.where(first, r0, r1) * g

    for i in range(4):
        at = slice(320 * i, 320 * (i + 1))
        tok = (tok_ours, tok_theirs)[i // 2]
        qkv = dot32(tok[320 * (i % 2) : 320 * (i % 2 + 1)], wall[...])
        q = head_norm(qkv[:, :256], gain[0:1])
        q0[at] = jnp.where(first, q, 0.0).astype(BF16)
        q1[at] = jnp.where(second, q, 0.0).astype(BF16)
        k0[at] = head_norm(qkv[:, 256:512], gain[1:2]).astype(BF16)
        v0[at] = qkv[:, 512:].astype(BF16)

    for i in range(4):
        at = slice(320 * i, 320 * (i + 1))
        a = dot32(softmax(dot_t(q0[at], k0[...])), v0[...])
        b = dot32(softmax(dot_t(q1[at], k0[...])), v0[...])
        att = jnp.where(first, a, b)[:, :PAIR]
        from_zh = core if i < 2 else 1 - core
        for j in range(8):
            out[from_zh * 16 + (i % 2) * 8 + j] = att[40 * j : 40 * (j + 1)].astype(BF16)


def spatial(place, gain, *operands):
    return pl.pallas_call(
        spatial_kernel,
        out_shape=jax.ShapeDtypeStruct((32, 40, PAIR), BF16),
        in_specs=[SMEM] + [VMEM] * 4,
        out_specs=VMEM,
        scratch_shapes=[pltpu.VMEM((D, 768), BF16)] + [pltpu.VMEM((1280, 256), BF16)] * 4,
        compiler_params=pltpu.CompilerParams(vmem_limit_bytes=48 * 2**20),
        cost_estimate=pl.CostEstimate(
            flops=5_000_000_000, bytes_accessed=5_000_000, transcendentals=3_300_000
        ),
    )(place, gain, *operands)


def temporal_kernel(mods, gain, seg, back, res, wts, out, wos, wa, wb, wot, sem):
    parts = [
        (pl.ds(D, D), slice(REST, REST + D), wos),
        (pl.ds(0, D), slice(0, CUT), wa),
        (pl.ds(D, D), slice(0, REST), wb),
        (pl.ds(D, D), slice(REST + D, REST + 2 * D), wot),
    ]
    waits = [
        pltpu.make_async_copy(wts.at[rows, cols], to, sem.at[i])
        for i, (rows, cols, to) in enumerate(parts)
    ]
    for copy in waits:
        copy.start()
    waits[0].wait()
    hidden = res[...].astype(F32) + mods[2:3] * dot32(back[...], wos[...])
    hidden = hidden.astype(BF16).astype(F32)
    modulated = modulate(hidden, mods[3:4], mods[4:5])
    waits[1].wait()
    qkv_a = dot32(modulated, wa[...])
    waits[2].wait()
    qkv_b = dot32(modulated, wb[...])
    q, k = qkv_a[:, :D], qkv_a[:, D : 2 * D]
    v = jnp.concatenate([qkv_a[:, 2 * D :], qkv_b], 1).astype(BF16)

    def head_norm(heads, g):
        square = heads * heads
        high = square.astype(BF16)
        low = (square - high.astype(F32)).astype(BF16)
        mean = (dot32(high, seg[...]) + dot32(low, seg[...])) * (1.0 / HDIM)
        r = lax.rsqrt(mean + 1e-06)
        r_high = r.astype(BF16)
        r_mid = (r - r_high.astype(F32)).astype(BF16)
        r_low = (r - r_high.astype(F32) - r_mid.astype(F32)).astype(BF16)
        wide = dot_t(r_high, seg[...]) + dot_t(r_mid, seg[...]) + dot_t(r_low, seg[...])
        return heads * wide * g

    q = head_norm(q, gain[0:1])
    k = head_norm(k, gain[1:2]).astype(BF16)
    row = lax.broadcasted_iota(jnp.int32, (160, 160), 0)
    col = lax.broadcasted_iota(jnp.int32, (160, 160), 1)
    apart = lax.rem(row, 5) != lax.rem(col, 5)
    tiles = [None] * (D // 128)
    for h in range(HEADS):
        lo, hi = HDIM * h, HDIM * (h + 1)
        t0, t1 = lo // 128, -(-hi // 128)
        lane = lax.broadcasted_iota(jnp.int32, (1, 128 * (t1 - t0)), 1) + 128 * t0
        inside = (lane >= lo) & (lane < hi)
        window = slice(128 * t0, 128 * t1)
        qh = jnp.where(inside, q[:, window], 0.0).astype(BF16)
        scores = jnp.where(apart, -1e30, dot_t(qh, k[:, window]))
        att = dot32(softmax(scores), v[:, window])
        att = jnp.where(inside, att, 0.0)
        for t in range(t0, t1):
            part = att[:, 128 * (t - t0) : 128 * (t - t0 + 1)]
            tiles[t] = part if tiles[t] is None else tiles[t] + part
    attended = jnp.concatenate(tiles, 1).astype(BF16)
    waits[3].wait()
    out[...] = (hidden + mods[5:6] * dot32(attended, wot[...])).astype(BF16)


def temporal(mods, gain, seg, back, res, wts):
    return pl.pallas_call(
        temporal_kernel,
        out_shape=jax.ShapeDtypeStruct((160, D), BF16),
        in_specs=[VMEM] * 5 + [ANY],
        out_specs=VMEM,
        scratch_shapes=[
            pltpu.VMEM((D, D), BF16),
            pltpu.VMEM((D, CUT), BF16),
            pltpu.VMEM((D, REST), BF16),
            pltpu.VMEM((D, D), BF16),
            pltpu.SemaphoreType.DMA((4,)),
        ],
        compiler_params=pltpu.CompilerParams(vmem_limit_bytes=40 * 2**20),
        cost_estimate=pl.CostEstimate(
            flops=1_800_000_000, bytes_accessed=15_000_000, transcendentals=500_000
        ),
    )(mods, gain, seg, back, res, wts)


def in_order(zh, mine, far):
    return jnp.concatenate([jnp.where(zh == 0, mine, far), jnp.where(zh == 0, far, mine)], 0)


def per_device(latent, mod_s, mod_t, gain, wqkv_s, wout_s, wqkv_t, wout_t):
    core = lax.axis_index("core")
    zh = lax.axis_index("zh")
    y = lax.axis_index("y")
    place = jnp.stack([y, core]).astype(jnp.int32)
    other = [(0, 1), (1, 0)]
    latent = latent.reshape(4, 40, D)

    pad = jnp.zeros((36, 2 * CUT - 5 * D), BF16)
    tail = jnp.concatenate([wqkv_t[:, CUT:], wout_s, wout_t, pad], 1)
    half_r = jnp.where(core == 0, wqkv_t[:, :CUT], tail)
    far_r = lax.ppermute(half_r, "zh", other)

    pieces = []
    for k in range(4):
        piece = lax.dynamic_index_in_dim(latent, (y + 4 - k) % 4, 0, keepdims=False)
        route = [
            ((c * 4 + (t + k) % 4) * 2 + z, (z * 4 + t) * 2 + c)
            for c in range(2)
            for t in range(4)
            for z in range(2)
        ]
        pieces.append(lax.ppermute(piece, ("core", "y", "zh"), route))

    by_pair = wqkv_s.reshape(36, 3, 4, 2, PAIR)
    half_s = lax.dynamic_index_in_dim(by_pair, core, 3, keepdims=False)
    half_s = half_s.transpose(2, 0, 1, 3).reshape(4, 36, 3 * PAIR)
    w_x = lax.all_to_all(half_s, "x", split_axis=0, concat_axis=0, tiled=True)
    w_far = lax.ppermute(w_x, "zh", other)
    far_r, w_far, pieces = lax.optimization_barrier((far_r, w_far, pieces))
    w_x = jnp.stack([jnp.where(zh == 0, w_x, w_far), jnp.where(zh == 0, w_far, w_x)], 1)
    w_x = jnp.broadcast_to(w_x.reshape(1, D // 4, 3 * PAIR), (4, D // 4, 3 * PAIR))
    w_y = lax.all_to_all(w_x, "y", split_axis=0, concat_axis=0, tiled=True)
    w_y = w_y.reshape(D, 3 * PAIR)

    both_r = in_order(zh, half_r, far_r)
    weights = lax.all_gather(both_r, ("core", "y", "x"), axis=0, tiled=True)

    copies = merge(place, mod_s, pieces).reshape(4, 160, D)
    ours = lax.all_to_all(copies, "x", split_axis=0, concat_axis=0, tiled=True).reshape(640, D)
    ours, w_y = lax.optimization_barrier((ours, w_y))
    theirs = lax.ppermute(ours, "core", other)
    home_in, ours = lax.optimization_barrier((latent, ours))
    home = lax.all_to_all(home_in, ("zl", "core"), split_axis=1, concat_axis=0, tiled=True)
    home = home.reshape(160, D)
    gain_s = jnp.pad(jnp.tile(gain[:2], (1, 2)), ((0, 0), (0, 256 - PAIR)))
    att = spatial(place, gain_s, ours, theirs, w_y)

    att = att.reshape(2, 4, 4, 4, 2, 5, PAIR).transpose(3, 0, 2, 1, 4, 5, 6)
    att = att.reshape(256, 5, PAIR)
    everyone = ("zl", "zh", "y", "x", "core")
    back = lax.all_to_all(att, everyone, split_axis=0, concat_axis=0, tiled=True)
    back = back.reshape(32, 8, 5, PAIR).transpose(0, 2, 1, 3).reshape(160, D)

    seg = (jnp.arange(D)[:, None] // HDIM == jnp.arange(128)[None]).astype(BF16)
    mods = jnp.concatenate([mod_s, mod_t], 0)
    mixed = temporal(mods, jnp.tile(gain[2:], (1, HEADS)), seg, back, home, weights)
    mixed = lax.all_to_all(
        mixed.reshape(32, 5, D), ("zl", "core"), split_axis=0, concat_axis=1, tiled=True
    )
    return mixed.reshape(4, 1, 40, D)


def solution(mesh):
    fine = Mesh(mesh.devices.reshape(4, 2, 4, 4, 2), ("zl", "core", "y", "x", "zh"))
    frame, row = ("zl", "core"), ("y", "x", "zh")
    in_specs = (
        P(frame, row, None, None),
        P(),
        P(),
        P(),
        P(row, None),
        P(row, None),
        P(row, None),
        P(row, None),
    )
    return jax.shard_map(
        per_device,
        mesh=fine,
        in_specs=in_specs,
        out_specs=P(frame, row, None, None),
        check_vma=False,
    )
```

```python
import jax
import jax.numpy as jnp
from jax import lax
from jax.experimental import pallas as pl
from jax.experimental.pallas import tpu as pltpu
from jax.sharding import Mesh
from jax.sharding import PartitionSpec as P

HEADS = 16
HDIM = 72
D = 1152
PAIR = 2 * HDIM
CUT = 2944
REST = 3 * D - CUT
SCALE = HDIM**-0.5
EXP2 = 1.4426950408889634
F32 = jnp.float32
BF16 = jnp.bfloat16
VMEM = pl.BlockSpec(memory_space=pltpu.VMEM)
SMEM = pl.BlockSpec(memory_space=pltpu.SMEM)
ANY = pl.BlockSpec(memory_space=pl.ANY)


def dot32(a, b):
    return jnp.dot(a, b, preferred_element_type=F32)


def dot_t(a, b):
    return lax.dot_general(a, b, (((1,), (1,)), ((), ())), preferred_element_type=F32)


def modulate(values, shift, scale):
    center = values - jnp.mean(values, -1, keepdims=True)
    variance = jnp.mean(center * center, -1, keepdims=True)
    return (center * lax.rsqrt(variance + 1e-06) * (1.0 + scale) + shift).astype(BF16)


def norm_kernel(mod, rows, out):
    normed = modulate(rows[...].astype(F32), mod[0:1], mod[1:2])
    for copy in range(4):
        out[copy] = normed


def norm_copies(mod, rows):
    return pl.pallas_call(
        norm_kernel,
        out_shape=jax.ShapeDtypeStruct((4, 4, 40, D), BF16),
        in_specs=[VMEM] * 2,
        out_specs=VMEM,
        cost_estimate=pl.CostEstimate(flops=4_000_000, bytes_accessed=2_000_000, transcendentals=0),
    )(mod, rows)


def softmax(scores):
    highest = jnp.max(scores, -1, keepdims=True)
    expo = jnp.exp2((scores - highest) * (SCALE * EXP2))
    return (expo * (1.0 / jnp.sum(expo, -1, keepdims=True))).astype(BF16)


def spatial_kernel(place, gain, tok_ours, tok_theirs, w0, w1, w2, w3, out, wall, q0, q1, k0, v0):
    y, own_zh = place[0], place[1]
    quarter = D // 4
    wall[...] = jnp.zeros_like(wall)
    for k, w in enumerate((w0, w1, w2, w3)):
        rows = pl.ds(pl.multiple_of(lax.rem(y + k, 4) * quarter, quarter), quarter)
        for part in range(3):
            wall[rows, 256 * part : 256 * part + PAIR] = w[:, PAIR * part : PAIR * (part + 1)]
    lane = lax.broadcasted_iota(jnp.int32, (1, 256), 1)
    first = lane < HDIM
    second = (lane >= HDIM) & (lane < PAIR)

    def head_norm(heads, g):
        square = heads * heads
        s0 = jnp.sum(jnp.where(first, square, 0.0), -1, keepdims=True)
        s1 = jnp.sum(jnp.where(first, 0.0, square), -1, keepdims=True)
        r0 = lax.rsqrt(s0 * (1.0 / HDIM) + 1e-06)
        r1 = lax.rsqrt(s1 * (1.0 / HDIM) + 1e-06)
        return heads * jnp.where(first, r0, r1) * g

    for i in range(4):
        at = slice(320 * i, 320 * (i + 1))
        tok = (tok_ours, tok_theirs)[i // 2]
        qkv = dot32(tok[320 * (i % 2) : 320 * (i % 2 + 1)], wall[...])
        q = head_norm(qkv[:, :256], gain[0:1])
        q0[at] = jnp.where(first, q, 0.0).astype(BF16)
        q1[at] = jnp.where(second, q, 0.0).astype(BF16)
        k0[at] = head_norm(qkv[:, 256:512], gain[1:2]).astype(BF16)
        v0[at] = qkv[:, 512:].astype(BF16)

    for i in range(4):
        at = slice(320 * i, 320 * (i + 1))
        a = dot32(softmax(dot_t(q0[at], k0[...])), v0[...])
        b = dot32(softmax(dot_t(q1[at], k0[...])), v0[...])
        att = jnp.where(first, a, b)[:, :PAIR]
        from_zh = own_zh if i < 2 else 1 - own_zh
        for j in range(8):
            out[from_zh * 16 + (i % 2) * 8 + j] = att[40 * j : 40 * (j + 1)].astype(BF16)


def spatial(place, gain, *operands):
    return pl.pallas_call(
        spatial_kernel,
        out_shape=jax.ShapeDtypeStruct((32, 40, PAIR), BF16),
        in_specs=[SMEM] + [VMEM] * 7,
        out_specs=VMEM,
        scratch_shapes=[pltpu.VMEM((D, 768), BF16)] + [pltpu.VMEM((1280, 256), BF16)] * 4,
        compiler_params=pltpu.CompilerParams(vmem_limit_bytes=48 * 2**20),
        cost_estimate=pl.CostEstimate(
            flops=5_000_000_000, bytes_accessed=5_000_000, transcendentals=3_300_000
        ),
    )(place, gain, *operands)


def temporal_kernel(mods, gain, seg, back, res, wts, out, wos, wa, wb, wot, sem):
    parts = [
        (pl.ds(D, D), slice(REST, REST + D), wos),
        (pl.ds(0, D), slice(0, CUT), wa),
        (pl.ds(D, D), slice(0, REST), wb),
        (pl.ds(D, D), slice(REST + D, REST + 2 * D), wot),
    ]
    waits = [
        pltpu.make_async_copy(wts.at[rows, cols], to, sem.at[i])
        for i, (rows, cols, to) in enumerate(parts)
    ]
    for copy in waits:
        copy.start()
    waits[0].wait()
    hidden = res[...].astype(F32) + mods[2:3] * dot32(back[...], wos[...])
    hidden = hidden.astype(BF16).astype(F32)
    modulated = modulate(hidden, mods[3:4], mods[4:5])
    waits[1].wait()
    qkv_a = dot32(modulated, wa[...])
    waits[2].wait()
    qkv_b = dot32(modulated, wb[...])
    q, k = qkv_a[:, :D], qkv_a[:, D : 2 * D]
    v = jnp.concatenate([qkv_a[:, 2 * D :], qkv_b], 1).astype(BF16)

    def head_norm(heads, g):
        square = heads * heads
        high = square.astype(BF16)
        low = (square - high.astype(F32)).astype(BF16)
        mean = (dot32(high, seg[...]) + dot32(low, seg[...])) * (1.0 / HDIM)
        r = lax.rsqrt(mean + 1e-06)
        r_high = r.astype(BF16)
        r_mid = (r - r_high.astype(F32)).astype(BF16)
        r_low = (r - r_high.astype(F32) - r_mid.astype(F32)).astype(BF16)
        wide = dot_t(r_high, seg[...]) + dot_t(r_mid, seg[...]) + dot_t(r_low, seg[...])
        return heads * wide * g

    q = head_norm(q, gain[0:1])
    k = head_norm(k, gain[1:2]).astype(BF16)
    row = lax.broadcasted_iota(jnp.int32, (160, 160), 0)
    col = lax.broadcasted_iota(jnp.int32, (160, 160), 1)
    apart = lax.rem(row, 5) != lax.rem(col, 5)
    tiles = [None] * (D // 128)
    for h in range(HEADS):
        lo, hi = HDIM * h, HDIM * (h + 1)
        t0, t1 = lo // 128, -(-hi // 128)
        lane = lax.broadcasted_iota(jnp.int32, (1, 128 * (t1 - t0)), 1) + 128 * t0
        inside = (lane >= lo) & (lane < hi)
        window = slice(128 * t0, 128 * t1)
        qh = jnp.where(inside, q[:, window], 0.0).astype(BF16)
        scores = jnp.where(apart, -1e30, dot_t(qh, k[:, window]))
        att = dot32(softmax(scores), v[:, window])
        att = jnp.where(inside, att, 0.0)
        for t in range(t0, t1):
            part = att[:, 128 * (t - t0) : 128 * (t - t0 + 1)]
            tiles[t] = part if tiles[t] is None else tiles[t] + part
    attended = jnp.concatenate(tiles, 1).astype(BF16)
    waits[3].wait()
    out[...] = (hidden + mods[5:6] * dot32(attended, wot[...])).astype(BF16)


def temporal(mods, gain, seg, back, res, wts):
    return pl.pallas_call(
        temporal_kernel,
        out_shape=jax.ShapeDtypeStruct((160, D), BF16),
        in_specs=[VMEM] * 5 + [ANY],
        out_specs=VMEM,
        scratch_shapes=[
            pltpu.VMEM((D, D), BF16),
            pltpu.VMEM((D, CUT), BF16),
            pltpu.VMEM((D, REST), BF16),
            pltpu.VMEM((D, D), BF16),
            pltpu.SemaphoreType.DMA((4,)),
        ],
        compiler_params=pltpu.CompilerParams(vmem_limit_bytes=40 * 2**20),
        cost_estimate=pl.CostEstimate(
            flops=1_800_000_000, bytes_accessed=15_000_000, transcendentals=500_000
        ),
    )(mods, gain, seg, back, res, wts)


def in_order(zh, mine, far):
    return jnp.concatenate([jnp.where(zh == 0, mine, far), jnp.where(zh == 0, far, mine)], 0)


def per_device(latent, mod_s, mod_t, gain, wqkv_s, wout_s, wqkv_t, wout_t):
    core = lax.axis_index("core")
    zh = lax.axis_index("zh")
    y = lax.axis_index("y")
    own_zh = lax.rem(zh + core + y // 2, 2)
    place = jnp.stack([y, own_zh]).astype(jnp.int32)
    other = [(0, 1), (1, 0)]
    latent = latent.reshape(4, 40, D)

    stay = lax.dynamic_slice_in_dim(latent, 2 * zh, 2, 0)
    leave = lax.dynamic_slice_in_dim(latent, 2 - 2 * zh, 2, 0)
    moved = lax.ppermute(leave, ("core", "zh"), [(i, 3 - i) for i in range(4)])

    pad = jnp.zeros((36, 2 * CUT - 5 * D), BF16)
    tail = jnp.concatenate([wqkv_t[:, CUT:], wout_s, wout_t, pad], 1)
    half_r = jnp.where(core == 0, wqkv_t[:, :CUT], tail)
    far_r = lax.ppermute(half_r, "zh", other)

    by_pair = wqkv_s.reshape(36, 3, 4, 2, PAIR)
    half_s = lax.dynamic_index_in_dim(by_pair, core, 3, keepdims=False)
    half_s = half_s.transpose(2, 0, 1, 3).reshape(4, 36, 3 * PAIR)
    w_x = lax.all_to_all(half_s, "x", split_axis=0, concat_axis=0, tiled=True)
    moved, w_x, far_r = lax.optimization_barrier((moved, w_x, far_r))
    w_far = lax.ppermute(w_x, "zh", other)
    frames = jnp.concatenate(
        [jnp.where(core == 0, stay, moved), jnp.where(core == 0, moved, stay)], 0
    )
    rows = lax.all_to_all(frames, "y", split_axis=0, concat_axis=0, tiled=True)
    w_far, rows = lax.optimization_barrier((w_far, rows))
    weights = lax.all_gather(in_order(zh, half_r, far_r), ("core", "y", "x"), axis=0, tiled=True)

    w_z = jnp.stack([jnp.where(zh == 0, w_x, w_far), jnp.where(zh == 0, w_far, w_x)], 1)
    w_z = w_z.reshape(D // 4, 3 * PAIR)
    w_y = [w_z] + [
        lax.ppermute(w_z, "y", [((i + k) % 4, i) for i in range(4)]) for k in (1, 2, 3)
    ]

    copies = norm_copies(mod_s, rows).reshape(4, 160, D)
    ours = lax.all_to_all(copies, "x", split_axis=0, concat_axis=0, tiled=True).reshape(640, D)
    ours, w_y = lax.optimization_barrier((ours, w_y))
    theirs = lax.ppermute(ours, "core", other)
    home_in, ours = lax.optimization_barrier((latent, ours))
    home = lax.all_to_all(home_in, ("zl", "core"), split_axis=1, concat_axis=0, tiled=True)
    home = home.reshape(160, D)
    gain_s = jnp.pad(jnp.tile(gain[:2], (1, 2)), ((0, 0), (0, 256 - PAIR)))
    att = spatial(place, gain_s, ours, theirs, *w_y)

    att = att.reshape(2, 4, 4, 4, 2, 5, PAIR).transpose(3, 0, 2, 1, 4, 5, 6)
    att = att.reshape(256, 5, PAIR)
    everyone = ("zl", "zh", "y", "x", "core")
    back = lax.all_to_all(att, everyone, split_axis=0, concat_axis=0, tiled=True)
    back = back.reshape(4, 2, 2, 2, 8, 5, PAIR).transpose(0, 2, 1, 3, 5, 4, 6).reshape(160, D)

    seg = (jnp.arange(D)[:, None] // HDIM == jnp.arange(128)[None]).astype(BF16)
    mods = jnp.concatenate([mod_s, mod_t], 0)
    mixed = temporal(mods, jnp.tile(gain[2:], (1, HEADS)), seg, back, home, weights)
    mixed = lax.all_to_all(
        mixed.reshape(32, 5, D), ("zl", "core"), split_axis=0, concat_axis=1, tiled=True
    )
    return mixed.reshape(4, 1, 40, D)


def solution(mesh):
    fine = Mesh(mesh.devices.reshape(4, 2, 4, 4, 2), ("zl", "core", "y", "x", "zh"))
    frame, row = ("zl", "core"), ("y", "x", "zh")
    in_specs = (
        P(frame, row, None, None),
        P(),
        P(),
        P(),
        P(row, None),
        P(row, None),
        P(row, None),
        P(row, None),
    )
    return jax.shard_map(
        per_device,
        mesh=fine,
        in_specs=in_specs,
        out_specs=P(frame, row, None, None),
        check_vma=False,
    )
```

```python
import jax
import jax.numpy as jnp
from jax import lax
from jax.experimental import pallas as pl
from jax.experimental.pallas import tpu as pltpu
from jax.sharding import Mesh
from jax.sharding import PartitionSpec as P

HEADS = 16
HDIM = 72
D = 1152
PAIR = 2 * HDIM
CUT = 2944
REST = 3 * D - CUT
SCALE = HDIM**-0.5
EXP2 = 1.4426950408889634
F32 = jnp.float32
BF16 = jnp.bfloat16
VMEM = pl.BlockSpec(memory_space=pltpu.VMEM)
SMEM = pl.BlockSpec(memory_space=pltpu.SMEM)
ANY = pl.BlockSpec(memory_space=pl.ANY)


def dot32(a, b):
    return jnp.dot(a, b, preferred_element_type=F32)


def dot_t(a, b):
    return lax.dot_general(a, b, (((1,), (1,)), ((), ())), preferred_element_type=F32)


def modulate(values, shift, scale):
    center = values - jnp.mean(values, -1, keepdims=True)
    variance = jnp.mean(center * center, -1, keepdims=True)
    return (center * lax.rsqrt(variance + 1e-06) * (1.0 + scale) + shift).astype(BF16)


def norm_kernel(mod, rows, out):
    normed = modulate(rows[...].astype(F32), mod[0:1], mod[1:2])
    for copy in range(4):
        out[copy] = normed


def norm_copies(mod, rows):
    return pl.pallas_call(
        norm_kernel,
        out_shape=jax.ShapeDtypeStruct((4, 4, 40, D), BF16),
        in_specs=[VMEM] * 2,
        out_specs=VMEM,
        cost_estimate=pl.CostEstimate(flops=4_000_000, bytes_accessed=2_000_000, transcendentals=0),
    )(mod, rows)


def softmax(scores):
    highest = jnp.max(scores, -1, keepdims=True)
    expo = jnp.exp2((scores - highest) * (SCALE * EXP2))
    return (expo * (1.0 / jnp.sum(expo, -1, keepdims=True))).astype(BF16)


def spatial_kernel(place, gain, tok_ours, tok_theirs, w0, w1, w2, w3, out, wall, q0, q1, k0, v0):
    y, own_zh = place[0], place[1]
    quarter = D // 4
    wall[...] = jnp.zeros_like(wall)
    for k, w in enumerate((w0, w1, w2, w3)):
        rows = pl.ds(pl.multiple_of(lax.rem(y + k, 4) * quarter, quarter), quarter)
        for part in range(3):
            wall[rows, 256 * part : 256 * part + PAIR] = w[:, PAIR * part : PAIR * (part + 1)]
    lane = lax.broadcasted_iota(jnp.int32, (1, 256), 1)
    first = lane < HDIM
    second = (lane >= HDIM) & (lane < PAIR)

    def head_norm(heads, g):
        square = heads * heads
        s0 = jnp.sum(jnp.where(first, square, 0.0), -1, keepdims=True)
        s1 = jnp.sum(jnp.where(first, 0.0, square), -1, keepdims=True)
        r0 = lax.rsqrt(s0 * (1.0 / HDIM) + 1e-06)
        r1 = lax.rsqrt(s1 * (1.0 / HDIM) + 1e-06)
        return heads * jnp.where(first, r0, r1) * g

    for i in range(4):
        at = slice(320 * i, 320 * (i + 1))
        tok = (tok_ours, tok_theirs)[i // 2]
        qkv = dot32(tok[320 * (i % 2) : 320 * (i % 2 + 1)], wall[...])
        q = head_norm(qkv[:, :256], gain[0:1])
        q0[at] = jnp.where(first, q, 0.0).astype(BF16)
        q1[at] = jnp.where(second, q, 0.0).astype(BF16)
        k0[at] = head_norm(qkv[:, 256:512], gain[1:2]).astype(BF16)
        v0[at] = jnp.where(lane == PAIR, 1.0, qkv[:, 512:]).astype(BF16)

    def attend(queries):
        scores = dot_t(queries, k0[...])
        highest = jnp.max(scores, -1, keepdims=True)
        expo = jnp.exp2((scores - highest) * (SCALE * EXP2)).astype(BF16)
        both = dot32(expo, v0[...])
        return both * (1.0 / both[:, PAIR : PAIR + 1])

    for i in range(4):
        at = slice(320 * i, 320 * (i + 1))
        att = jnp.where(first, attend(q0[at]), attend(q1[at]))[:, :PAIR]
        from_zh = own_zh if i < 2 else 1 - own_zh
        for j in range(8):
            out[from_zh * 16 + (i % 2) * 8 + j] = att[40 * j : 40 * (j + 1)].astype(BF16)


def spatial(place, gain, *operands):
    return pl.pallas_call(
        spatial_kernel,
        out_shape=jax.ShapeDtypeStruct((32, 40, PAIR), BF16),
        in_specs=[SMEM] + [VMEM] * 7,
        out_specs=VMEM,
        scratch_shapes=[pltpu.VMEM((D, 768), BF16)] + [pltpu.VMEM((1280, 256), BF16)] * 4,
        compiler_params=pltpu.CompilerParams(vmem_limit_bytes=48 * 2**20),
        cost_estimate=pl.CostEstimate(
            flops=5_000_000_000, bytes_accessed=5_000_000, transcendentals=3_300_000
        ),
    )(place, gain, *operands)


def temporal_kernel(mods, gain, seg, back, res, wts, out, wos, wq, wk, wv, wot, sem):
    parts = [
        (pl.ds(D, D), slice(REST, REST + D), wos),
        (pl.ds(0, D), slice(0, D), wq),
        (pl.ds(0, D), slice(D, 2 * D), wk),
        (pl.ds(0, D), slice(2 * D, CUT), wv.at[:, : CUT - 2 * D]),
        (pl.ds(D, D), slice(0, REST), wv.at[:, CUT - 2 * D :]),
        (pl.ds(D, D), slice(REST + D, REST + 2 * D), wot),
    ]
    waits = [
        pltpu.make_async_copy(wts.at[rows, cols], to, sem.at[i])
        for i, (rows, cols, to) in enumerate(parts)
    ]
    for copy in waits:
        copy.start()
    waits[0].wait()
    hidden = res[...].astype(F32) + mods[2:3] * dot32(back[...], wos[...])
    hidden = hidden.astype(BF16).astype(F32)
    modulated = modulate(hidden, mods[3:4], mods[4:5])

    def head_norm(heads, g):
        square = heads * heads
        high = square.astype(BF16)
        low = (square - high.astype(F32)).astype(BF16)
        mean = (dot32(high, seg[...]) + dot32(low, seg[...])) * (1.0 / HDIM)
        r = lax.rsqrt(mean + 1e-06)
        r_high = r.astype(BF16)
        r_mid = (r - r_high.astype(F32)).astype(BF16)
        r_low = (r - r_high.astype(F32) - r_mid.astype(F32)).astype(BF16)
        wide = dot_t(r_high, seg[...]) + dot_t(r_mid, seg[...]) + dot_t(r_low, seg[...])
        return heads * wide * g

    waits[1].wait()
    q = head_norm(dot32(modulated, wq[...]), gain[0:1])
    waits[2].wait()
    k = head_norm(dot32(modulated, wk[...]), gain[1:2]).astype(BF16)
    waits[3].wait()
    waits[4].wait()
    v = dot32(modulated, wv[...]).astype(BF16)
    row = lax.broadcasted_iota(jnp.int32, (160, 160), 0)
    col = lax.broadcasted_iota(jnp.int32, (160, 160), 1)
    apart = row // 32 != col // 32
    tiles = [None] * (D // 128)
    for h in range(HEADS):
        lo, hi = HDIM * h, HDIM * (h + 1)
        t0, t1 = lo // 128, -(-hi // 128)
        lane = lax.broadcasted_iota(jnp.int32, (1, 128 * (t1 - t0)), 1) + 128 * t0
        inside = (lane >= lo) & (lane < hi)
        window = slice(128 * t0, 128 * t1)
        qh = jnp.where(inside, q[:, window], 0.0).astype(BF16)
        scores = jnp.where(apart, -1e30, dot_t(qh, k[:, window]))
        att = dot32(softmax(scores), v[:, window])
        att = jnp.where(inside, att, 0.0)
        for t in range(t0, t1):
            part = att[:, 128 * (t - t0) : 128 * (t - t0 + 1)]
            tiles[t] = part if tiles[t] is None else tiles[t] + part
    attended = jnp.concatenate(tiles, 1).astype(BF16)
    waits[5].wait()
    mixed = hidden + mods[5:6] * dot32(attended, wot[...])
    for p in range(5):
        for f in range(8):
            lo = 32 * p + 4 * f
            out[f, p] = mixed[lo : lo + 4].astype(BF16)


def temporal(mods, gain, seg, back, res, wts):
    return pl.pallas_call(
        temporal_kernel,
        out_shape=jax.ShapeDtypeStruct((8, 5, 4, D), BF16),
        in_specs=[VMEM] * 5 + [ANY],
        out_specs=VMEM,
        scratch_shapes=[
            pltpu.VMEM((D, D), BF16),
            pltpu.VMEM((D, D), BF16),
            pltpu.VMEM((D, D), BF16),
            pltpu.VMEM((D, D), BF16),
            pltpu.VMEM((D, D), BF16),
            pltpu.SemaphoreType.DMA((6,)),
        ],
        compiler_params=pltpu.CompilerParams(vmem_limit_bytes=40 * 2**20),
        cost_estimate=pl.CostEstimate(
            flops=1_800_000_000, bytes_accessed=15_000_000, transcendentals=500_000
        ),
    )(mods, gain, seg, back, res, wts)


def in_order(zh, mine, far):
    return jnp.concatenate([jnp.where(zh == 0, mine, far), jnp.where(zh == 0, far, mine)], 0)


def per_device(latent, mod_s, mod_t, gain, wqkv_s, wout_s, wqkv_t, wout_t):
    core = lax.axis_index("core")
    zh = lax.axis_index("zh")
    y = lax.axis_index("y")
    own_zh = lax.rem(zh + core + y // 2, 2)
    place = jnp.stack([y, own_zh]).astype(jnp.int32)
    other = [(0, 1), (1, 0)]
    latent = latent.reshape(4, 40, D)

    stay = lax.dynamic_slice_in_dim(latent, 2 * zh, 2, 0)
    leave = lax.dynamic_slice_in_dim(latent, 2 - 2 * zh, 2, 0)
    moved = lax.ppermute(leave, ("core", "zh"), [(i, 3 - i) for i in range(4)])

    pad = jnp.zeros((36, 2 * CUT - 5 * D), BF16)
    tail = jnp.concatenate([wqkv_t[:, CUT:], wout_s, wout_t, pad], 1)
    half_r = jnp.where(core == 0, wqkv_t[:, :CUT], tail)
    far_r = lax.ppermute(half_r, "zh", other)

    by_pair = wqkv_s.reshape(36, 3, 4, 2, PAIR)
    half_s = lax.dynamic_index_in_dim(by_pair, core, 3, keepdims=False)
    half_s = half_s.transpose(2, 0, 1, 3).reshape(4, 36, 3 * PAIR)
    w_x = lax.all_to_all(half_s, "x", split_axis=0, concat_axis=0, tiled=True)
    moved, w_x, far_r = lax.optimization_barrier((moved, w_x, far_r))
    w_far = lax.ppermute(w_x, "zh", other)
    frames = jnp.concatenate(
        [jnp.where(core == 0, stay, moved), jnp.where(core == 0, moved, stay)], 0
    )
    rows = lax.all_to_all(frames, "y", split_axis=0, concat_axis=0, tiled=True)
    by_home = latent.reshape(4, 8, 5, D).transpose(1, 2, 0, 3)
    w_far, rows, by_home = lax.optimization_barrier((w_far, rows, by_home))
    weights = lax.all_gather(in_order(zh, half_r, far_r), ("core", "y", "x"), axis=0, tiled=True)

    w_z = jnp.stack([jnp.where(zh == 0, w_x, w_far), jnp.where(zh == 0, w_far, w_x)], 1)
    w_z = w_z.reshape(D // 4, 3 * PAIR)
    w_y = [w_z] + [
        lax.ppermute(w_z, "y", [((i + k) % 4, i) for i in range(4)]) for k in (1, 2, 3)
    ]

    copies = norm_copies(mod_s, rows).reshape(4, 160, D)
    ours = lax.all_to_all(copies, "x", split_axis=0, concat_axis=0, tiled=True).reshape(640, D)
    ours, w_y = lax.optimization_barrier((ours, w_y))
    theirs = lax.ppermute(ours, "core", other)
    by_home, ours = lax.optimization_barrier((by_home, ours))
    home = lax.all_to_all(by_home, ("zl", "core"), split_axis=0, concat_axis=0, tiled=True)
    home = home.transpose(1, 0, 2, 3).reshape(160, D)
    gain_s = jnp.pad(jnp.tile(gain[:2], (1, 2)), ((0, 0), (0, 256 - PAIR)))
    att = spatial(place, gain_s, ours, theirs, *w_y)

    att = att.reshape(2, 4, 4, 4, 2, 5, PAIR).transpose(3, 0, 2, 1, 4, 5, 6)
    att = att.reshape(256, 5, PAIR)
    everyone = ("zl", "zh", "y", "x", "core")
    back = lax.all_to_all(att, everyone, split_axis=0, concat_axis=0, tiled=True)
    back = back.reshape(4, 2, 2, 2, 8, 5, PAIR).transpose(5, 0, 2, 1, 3, 4, 6).reshape(160, D)

    seg = (jnp.arange(D)[:, None] // HDIM == jnp.arange(128)[None]).astype(BF16)
    mods = jnp.concatenate([mod_s, mod_t], 0)
    mixed = temporal(mods, jnp.tile(gain[2:], (1, HEADS)), seg, back, home, weights)
    mixed = lax.all_to_all(mixed, ("zl", "core"), split_axis=0, concat_axis=0, tiled=True)
    return mixed.transpose(2, 0, 1, 3).reshape(4, 1, 40, D)


def solution(mesh):
    fine = Mesh(mesh.devices.reshape(4, 2, 4, 4, 2), ("zl", "core", "y", "x", "zh"))
    frame, row = ("zl", "core"), ("y", "x", "zh")
    in_specs = (
        P(frame, row, None, None),
        P(),
        P(),
        P(),
        P(row, None),
        P(row, None),
        P(row, None),
        P(row, None),
    )
    return jax.shard_map(
        per_device,
        mesh=fine,
        in_specs=in_specs,
        out_specs=P(frame, row, None, None),
        check_vma=False,
    )
```

```python
import jax
import jax.numpy as jnp
from jax import lax
from jax.experimental import pallas as pl
from jax.experimental.pallas import tpu as pltpu
from jax.sharding import Mesh
from jax.sharding import PartitionSpec as P

HEADS = 16
HDIM = 72
D = 1152
PAIR = 2 * HDIM
CUT = 2944
REST = 3 * D - CUT
SCALE = HDIM**-0.5
EXP2 = 1.4426950408889634
F32 = jnp.float32
BF16 = jnp.bfloat16
VMEM = pl.BlockSpec(memory_space=pltpu.VMEM)
SMEM = pl.BlockSpec(memory_space=pltpu.SMEM)
ANY = pl.BlockSpec(memory_space=pl.ANY)


def dot32(a, b):
    return jnp.dot(a, b, preferred_element_type=F32)


def dot_t(a, b):
    return lax.dot_general(a, b, (((1,), (1,)), ((), ())), preferred_element_type=F32)


def modulate(values, shift, scale):
    center = values - jnp.mean(values, -1, keepdims=True)
    variance = jnp.mean(center * center, -1, keepdims=True)
    return (center * lax.rsqrt(variance + 1e-06) * (1.0 + scale) + shift).astype(BF16)


def norm_kernel(mod, rows, out):
    normed = modulate(rows[...].astype(F32), mod[0:1], mod[1:2])
    for copy in range(4):
        out[copy] = normed


def norm_copies(mod, rows):
    return pl.pallas_call(
        norm_kernel,
        out_shape=jax.ShapeDtypeStruct((4, 4, 40, D), BF16),
        in_specs=[VMEM] * 2,
        out_specs=VMEM,
        compiler_params=pltpu.CompilerParams(vmem_limit_bytes=12 * 2**20),
        cost_estimate=pl.CostEstimate(flops=4_000_000, bytes_accessed=2_000_000, transcendentals=0),
    )(mod, rows)


def softmax(scores):
    highest = jnp.max(scores, -1, keepdims=True)
    expo = jnp.exp2((scores - highest) * (SCALE * EXP2))
    return (expo * (1.0 / jnp.sum(expo, -1, keepdims=True))).astype(BF16)


def spatial_kernel(place, gain, tok_ours, tok_theirs, w0, w1, w2, w3, out, wall, q0, q1, k0, v0):
    y, own_zh = place[0], place[1]
    quarter = D // 4
    wall[...] = jnp.zeros_like(wall)
    for k, w in enumerate((w0, w1, w2, w3)):
        rows = pl.ds(pl.multiple_of(lax.rem(y + k, 4) * quarter, quarter), quarter)
        for part in range(3):
            wall[rows, 256 * part : 256 * part + PAIR] = w[:, PAIR * part : PAIR * (part + 1)]
    lane = lax.broadcasted_iota(jnp.int32, (1, 256), 1)
    first = lane < HDIM
    second = (lane >= HDIM) & (lane < PAIR)

    def head_norm(heads, g):
        square = heads * heads
        s0 = jnp.sum(jnp.where(first, square, 0.0), -1, keepdims=True)
        s1 = jnp.sum(jnp.where(first, 0.0, square), -1, keepdims=True)
        r0 = lax.rsqrt(s0 * (1.0 / HDIM) + 1e-06)
        r1 = lax.rsqrt(s1 * (1.0 / HDIM) + 1e-06)
        return heads * jnp.where(first, r0, r1) * g

    for i in range(4):
        at = slice(320 * i, 320 * (i + 1))
        tok = (tok_ours, tok_theirs)[i // 2]
        qkv = dot32(tok[320 * (i % 2) : 320 * (i % 2 + 1)], wall[...])
        q = head_norm(qkv[:, :256], gain[0:1])
        q0[at] = jnp.where(first, q, 0.0).astype(BF16)
        q1[at] = jnp.where(second, q, 0.0).astype(BF16)
        k0[at] = head_norm(qkv[:, 256:512], gain[1:2]).astype(BF16)
        v0[at] = jnp.where(lane == PAIR, 1.0, qkv[:, 512:]).astype(BF16)

    def attend(queries):
        scores = dot_t(queries, k0[...])
        highest = jnp.max(scores, -1, keepdims=True)
        expo = jnp.exp2((scores - highest) * (SCALE * EXP2)).astype(BF16)
        both = dot32(expo, v0[...])
        return both * (1.0 / both[:, PAIR : PAIR + 1])

    for i in range(4):
        at = slice(320 * i, 320 * (i + 1))
        att = jnp.where(first, attend(q0[at]), attend(q1[at]))[:, :PAIR]
        from_zh = own_zh if i < 2 else 1 - own_zh
        for j in range(8):
            out[from_zh * 16 + (i % 2) * 8 + j] = att[40 * j : 40 * (j + 1)].astype(BF16)


def spatial(place, gain, *operands):
    return pl.pallas_call(
        spatial_kernel,
        out_shape=jax.ShapeDtypeStruct((32, 40, PAIR), BF16),
        in_specs=[SMEM] + [VMEM] * 7,
        out_specs=VMEM,
        scratch_shapes=[pltpu.VMEM((D, 768), BF16)] + [pltpu.VMEM((1280, 256), BF16)] * 4,
        compiler_params=pltpu.CompilerParams(vmem_limit_bytes=48 * 2**20),
        cost_estimate=pl.CostEstimate(
            flops=5_000_000_000, bytes_accessed=5_000_000, transcendentals=3_300_000
        ),
    )(place, gain, *operands)


def temporal_kernel(mods, gain, seg, back, res, wts, out, wos, wq, wk, wv, wot, sem):
    parts = [
        (pl.ds(D, D), slice(REST, REST + D), wos),
        (pl.ds(0, D), slice(0, D), wq),
        (pl.ds(0, D), slice(D, 2 * D), wk),
        (pl.ds(0, D), slice(2 * D, CUT), wv.at[:, : CUT - 2 * D]),
        (pl.ds(D, D), slice(0, REST), wv.at[:, CUT - 2 * D :]),
        (pl.ds(D, D), slice(REST + D, REST + 2 * D), wot),
    ]
    waits = [
        pltpu.make_async_copy(wts.at[rows, cols], to, sem.at[i])
        for i, (rows, cols, to) in enumerate(parts)
    ]
    for copy in waits:
        copy.start()
    waits[0].wait()
    hidden = res[...].astype(F32) + mods[2:3] * dot32(back[...], wos[...])
    hidden = hidden.astype(BF16).astype(F32)
    modulated = modulate(hidden, mods[3:4], mods[4:5])

    def head_norm(heads, g):
        square = heads * heads
        high = square.astype(BF16)
        low = (square - high.astype(F32)).astype(BF16)
        mean = (dot32(high, seg[...]) + dot32(low, seg[...])) * (1.0 / HDIM)
        r = lax.rsqrt(mean + 1e-06)
        r_high = r.astype(BF16)
        r_mid = (r - r_high.astype(F32)).astype(BF16)
        r_low = (r - r_high.astype(F32) - r_mid.astype(F32)).astype(BF16)
        wide = dot_t(r_high, seg[...]) + dot_t(r_mid, seg[...]) + dot_t(r_low, seg[...])
        return heads * wide * g

    waits[1].wait()
    q = head_norm(dot32(modulated, wq[...]), gain[0:1])
    waits[2].wait()
    k = head_norm(dot32(modulated, wk[...]), gain[1:2]).astype(BF16)
    waits[3].wait()
    waits[4].wait()
    v = dot32(modulated, wv[...]).astype(BF16)
    row = lax.broadcasted_iota(jnp.int32, (160, 160), 0)
    col = lax.broadcasted_iota(jnp.int32, (160, 160), 1)
    apart = row // 32 != col // 32
    tiles = [None] * (D // 128)
    for h in range(HEADS):
        lo, hi = HDIM * h, HDIM * (h + 1)
        t0, t1 = lo // 128, -(-hi // 128)
        lane = lax.broadcasted_iota(jnp.int32, (1, 128 * (t1 - t0)), 1) + 128 * t0
        inside = (lane >= lo) & (lane < hi)
        window = slice(128 * t0, 128 * t1)
        qh = jnp.where(inside, q[:, window], 0.0).astype(BF16)
        scores = jnp.where(apart, -1e30, dot_t(qh, k[:, window]))
        att = dot32(softmax(scores), v[:, window])
        att = jnp.where(inside, att, 0.0)
        for t in range(t0, t1):
            part = att[:, 128 * (t - t0) : 128 * (t - t0 + 1)]
            tiles[t] = part if tiles[t] is None else tiles[t] + part
    attended = jnp.concatenate(tiles, 1).astype(BF16)
    waits[5].wait()
    mixed = hidden + mods[5:6] * dot32(attended, wot[...])
    for p in range(5):
        for f in range(8):
            lo = 32 * p + 4 * f
            out[f, p] = mixed[lo : lo + 4].astype(BF16)


def temporal(mods, gain, seg, back, res, wts):
    return pl.pallas_call(
        temporal_kernel,
        out_shape=jax.ShapeDtypeStruct((8, 5, 4, D), BF16),
        in_specs=[VMEM] * 5 + [ANY],
        out_specs=VMEM,
        scratch_shapes=[
            pltpu.VMEM((D, D), BF16),
            pltpu.VMEM((D, D), BF16),
            pltpu.VMEM((D, D), BF16),
            pltpu.VMEM((D, D), BF16),
            pltpu.VMEM((D, D), BF16),
            pltpu.SemaphoreType.DMA((6,)),
        ],
        compiler_params=pltpu.CompilerParams(vmem_limit_bytes=40 * 2**20),
        cost_estimate=pl.CostEstimate(
            flops=1_800_000_000, bytes_accessed=15_000_000, transcendentals=500_000
        ),
    )(mods, gain, seg, back, res, wts)


def in_order(zh, mine, far):
    return jnp.concatenate([jnp.where(zh == 0, mine, far), jnp.where(zh == 0, far, mine)], 0)


def per_device(latent, mod_s, mod_t, gain, wqkv_s, wout_s, wqkv_t, wout_t):
    core = lax.axis_index("core")
    zh = lax.axis_index("zh")
    y = lax.axis_index("y")
    own_zh = lax.rem(zh + core + y // 2, 2)
    place = jnp.stack([y, own_zh]).astype(jnp.int32)
    other = [(0, 1), (1, 0)]
    latent = latent.reshape(4, 40, D)

    stay = lax.dynamic_slice_in_dim(latent, 2 * zh, 2, 0)
    leave = lax.dynamic_slice_in_dim(latent, 2 - 2 * zh, 2, 0)
    moved = lax.ppermute(leave, ("core", "zh"), [(i, 3 - i) for i in range(4)])

    pad = jnp.zeros((36, 2 * CUT - 5 * D), BF16)
    tail = jnp.concatenate([wqkv_t[:, CUT:], wout_s, wout_t, pad], 1)
    half_r = jnp.where(core == 0, wqkv_t[:, :CUT], tail)
    far_r = lax.ppermute(half_r, "zh", other)

    by_pair = wqkv_s.reshape(36, 3, 4, 2, PAIR)
    half_s = lax.dynamic_index_in_dim(by_pair, core, 3, keepdims=False)
    half_s = half_s.transpose(2, 0, 1, 3).reshape(4, 36, 3 * PAIR)
    w_x = lax.all_to_all(half_s, "x", split_axis=0, concat_axis=0, tiled=True)
    moved, w_x, far_r = lax.optimization_barrier((moved, w_x, far_r))
    w_far = lax.ppermute(w_x, "zh", other)
    frames = jnp.concatenate(
        [jnp.where(core == 0, stay, moved), jnp.where(core == 0, moved, stay)], 0
    )
    rows = lax.all_to_all(frames, "y", split_axis=0, concat_axis=0, tiled=True)
    by_home = latent.reshape(4, 8, 5, D).transpose(1, 2, 0, 3)
    rows, by_home = lax.optimization_barrier((rows, by_home))
    copies = norm_copies(mod_s, rows).reshape(4, 160, D)
    copies, w_far = lax.optimization_barrier((copies, w_far))
    weights = lax.all_gather(in_order(zh, half_r, far_r), ("core", "y", "x"), axis=0, tiled=True)

    w_z = jnp.stack([jnp.where(zh == 0, w_x, w_far), jnp.where(zh == 0, w_far, w_x)], 1)
    w_z = w_z.reshape(D // 4, 3 * PAIR)
    w_y = [w_z] + [
        lax.ppermute(w_z, "y", [((i + k) % 4, i) for i in range(4)]) for k in (1, 2, 3)
    ]

    ours = lax.all_to_all(copies, "x", split_axis=0, concat_axis=0, tiled=True).reshape(640, D)
    ours, w_y = lax.optimization_barrier((ours, w_y))
    theirs = lax.ppermute(ours, "core", other)
    by_home, ours = lax.optimization_barrier((by_home, ours))
    home = lax.all_to_all(by_home, ("zl", "core"), split_axis=0, concat_axis=0, tiled=True)
    home = home.transpose(1, 0, 2, 3).reshape(160, D)
    gain_s = jnp.pad(jnp.tile(gain[:2], (1, 2)), ((0, 0), (0, 256 - PAIR)))
    att = spatial(place, gain_s, ours, theirs, *w_y)

    att = att.reshape(2, 4, 4, 4, 2, 5, PAIR).transpose(3, 0, 2, 1, 4, 5, 6)
    att = att.reshape(256, 5, PAIR)
    everyone = ("zl", "zh", "y", "x", "core")
    back = lax.all_to_all(att, everyone, split_axis=0, concat_axis=0, tiled=True)
    back = back.reshape(4, 2, 2, 2, 8, 5, PAIR).transpose(5, 0, 2, 1, 3, 4, 6).reshape(160, D)

    seg = (jnp.arange(D)[:, None] // HDIM == jnp.arange(128)[None]).astype(BF16)
    mods = jnp.concatenate([mod_s, mod_t], 0)
    mixed = temporal(mods, jnp.tile(gain[2:], (1, HEADS)), seg, back, home, weights)
    mixed = lax.all_to_all(mixed, ("zl", "core"), split_axis=0, concat_axis=0, tiled=True)
    return mixed.transpose(2, 0, 1, 3).reshape(4, 1, 40, D)


def solution(mesh):
    fine = Mesh(mesh.devices.reshape(4, 2, 4, 4, 2), ("zl", "core", "y", "x", "zh"))
    frame, row = ("zl", "core"), ("y", "x", "zh")
    in_specs = (
        P(frame, row, None, None),
        P(),
        P(),
        P(),
        P(row, None),
        P(row, None),
        P(row, None),
        P(row, None),
    )
    return jax.shard_map(
        per_device,
        mesh=fine,
        in_specs=in_specs,
        out_specs=P(frame, row, None, None),
        check_vma=False,
    )
```

```python
import jax
import jax.numpy as jnp
from jax import lax
from jax.experimental import pallas as pl
from jax.experimental.pallas import tpu as pltpu
from jax.sharding import Mesh
from jax.sharding import PartitionSpec as P

HEADS = 16
HDIM = 72
D = 1152
PAIR = 2 * HDIM
CUT = 2944
REST = 3 * D - CUT
SCALE = HDIM**-0.5
EXP2 = 1.4426950408889634
F32 = jnp.float32
BF16 = jnp.bfloat16
VMEM = pl.BlockSpec(memory_space=pltpu.VMEM)
SMEM = pl.BlockSpec(memory_space=pltpu.SMEM)
ANY = pl.BlockSpec(memory_space=pl.ANY)


def dot32(a, b):
    return jnp.dot(a, b, preferred_element_type=F32)


def dot_t(a, b):
    return lax.dot_general(a, b, (((1,), (1,)), ((), ())), preferred_element_type=F32)


def modulate(values, shift, scale):
    center = values - jnp.mean(values, -1, keepdims=True)
    variance = jnp.mean(center * center, -1, keepdims=True)
    return (center * lax.rsqrt(variance + 1e-06) * (1.0 + scale) + shift).astype(BF16)


def norm_kernel(mod, rows, out):
    normed = modulate(rows[...].astype(F32), mod[0:1], mod[1:2])
    for copy in range(4):
        out[copy] = normed


def norm_copies(mod, rows):
    return pl.pallas_call(
        norm_kernel,
        out_shape=jax.ShapeDtypeStruct((4, 4, 40, D), BF16),
        in_specs=[VMEM] * 2,
        out_specs=VMEM,
        cost_estimate=pl.CostEstimate(flops=4_000_000, bytes_accessed=2_000_000, transcendentals=0),
    )(mod, rows)


def softmax(scores):
    highest = jnp.max(scores, -1, keepdims=True)
    expo = jnp.exp2((scores - highest) * (SCALE * EXP2))
    return (expo * (1.0 / jnp.sum(expo, -1, keepdims=True))).astype(BF16)


def spatial_kernel(place, gain, tok_ours, tok_theirs, w0, w1, w2, w3, out, wall, q0, q1, k0, v0):
    y, own_zh = place[0], place[1]
    quarter = D // 4
    wall[...] = jnp.zeros_like(wall)
    for k, w in enumerate((w0, w1, w2, w3)):
        rows = pl.ds(pl.multiple_of(lax.rem(y + k, 4) * quarter, quarter), quarter)
        for part in range(3):
            wall[rows, 256 * part : 256 * part + PAIR] = w[:, PAIR * part : PAIR * (part + 1)]
    lane = lax.broadcasted_iota(jnp.int32, (1, 256), 1)
    first = lane < HDIM
    second = (lane >= HDIM) & (lane < PAIR)

    def head_norm(heads, g):
        square = heads * heads
        s0 = jnp.sum(jnp.where(first, square, 0.0), -1, keepdims=True)
        s1 = jnp.sum(jnp.where(first, 0.0, square), -1, keepdims=True)
        r0 = lax.rsqrt(s0 * (1.0 / HDIM) + 1e-06)
        r1 = lax.rsqrt(s1 * (1.0 / HDIM) + 1e-06)
        return heads * jnp.where(first, r0, r1) * g

    for i in range(4):
        at = slice(320 * i, 320 * (i + 1))
        tok = (tok_ours, tok_theirs)[i // 2]
        qkv = dot32(tok[320 * (i % 2) : 320 * (i % 2 + 1)], wall[...])
        q = head_norm(qkv[:, :256], gain[0:1])
        q0[at] = jnp.where(first, q, 0.0).astype(BF16)
        q1[at] = jnp.where(second, q, 0.0).astype(BF16)
        k0[at] = head_norm(qkv[:, 256:512], gain[1:2]).astype(BF16)
        v0[at] = jnp.where(lane == PAIR, 1.0, qkv[:, 512:]).astype(BF16)

    def attend(queries):
        scores = dot_t(queries, k0[...])
        highest = jnp.max(scores, -1, keepdims=True)
        expo = jnp.exp2((scores - highest) * (SCALE * EXP2)).astype(BF16)
        both = dot32(expo, v0[...])
        return both * (1.0 / both[:, PAIR : PAIR + 1])

    for i in range(4):
        at = slice(320 * i, 320 * (i + 1))
        att = jnp.where(first, attend(q0[at]), attend(q1[at]))[:, :PAIR]
        from_zh = own_zh if i < 2 else 1 - own_zh
        for j in range(8):
            out[from_zh * 16 + (i % 2) * 8 + j] = att[40 * j : 40 * (j + 1)].astype(BF16)


def spatial(place, gain, *operands):
    return pl.pallas_call(
        spatial_kernel,
        out_shape=jax.ShapeDtypeStruct((32, 40, PAIR), BF16),
        in_specs=[SMEM] + [VMEM] * 7,
        out_specs=VMEM,
        scratch_shapes=[pltpu.VMEM((D, 768), BF16)] + [pltpu.VMEM((1280, 256), BF16)] * 4,
        compiler_params=pltpu.CompilerParams(vmem_limit_bytes=48 * 2**20),
        cost_estimate=pl.CostEstimate(
            flops=5_000_000_000, bytes_accessed=5_000_000, transcendentals=3_300_000
        ),
    )(place, gain, *operands)


def temporal_kernel(mods, gain, seg, back, res, wts, out, wos, wq, wk, wv, wot, sem):
    parts = [
        (pl.ds(D, D), slice(REST, REST + D), wos),
        (pl.ds(0, D), slice(0, D), wq),
        (pl.ds(0, D), slice(D, 2 * D), wk),
        (pl.ds(0, D), slice(2 * D, CUT), wv.at[:, : CUT - 2 * D]),
        (pl.ds(D, D), slice(0, REST), wv.at[:, CUT - 2 * D :]),
        (pl.ds(D, D), slice(REST + D, REST + 2 * D), wot),
    ]
    waits = [
        pltpu.make_async_copy(wts.at[rows, cols], to, sem.at[i])
        for i, (rows, cols, to) in enumerate(parts)
    ]
    for copy in waits:
        copy.start()
    waits[0].wait()
    hidden = res[...].astype(F32) + mods[2:3] * dot32(back[...], wos[...])
    hidden = hidden.astype(BF16).astype(F32)
    modulated = modulate(hidden, mods[3:4], mods[4:5])

    def head_norm(heads, g):
        square = heads * heads
        high = square.astype(BF16)
        low = (square - high.astype(F32)).astype(BF16)
        mean = (dot32(high, seg[...]) + dot32(low, seg[...])) * (1.0 / HDIM)
        r = lax.rsqrt(mean + 1e-06)
        r_high = r.astype(BF16)
        r_mid = (r - r_high.astype(F32)).astype(BF16)
        r_low = (r - r_high.astype(F32) - r_mid.astype(F32)).astype(BF16)
        wide = dot_t(r_high, seg[...]) + dot_t(r_mid, seg[...]) + dot_t(r_low, seg[...])
        return heads * wide * g

    waits[1].wait()
    q = head_norm(dot32(modulated, wq[...]), gain[0:1])
    waits[2].wait()
    k = head_norm(dot32(modulated, wk[...]), gain[1:2]).astype(BF16)
    waits[3].wait()
    waits[4].wait()
    v = dot32(modulated, wv[...]).astype(BF16)
    row = lax.broadcasted_iota(jnp.int32, (160, 160), 0)
    col = lax.broadcasted_iota(jnp.int32, (160, 160), 1)
    apart = row // 32 != col // 32
    tiles = [None] * (D // 128)
    for h in range(HEADS):
        lo, hi = HDIM * h, HDIM * (h + 1)
        t0, t1 = lo // 128, -(-hi // 128)
        lane = lax.broadcasted_iota(jnp.int32, (1, 128 * (t1 - t0)), 1) + 128 * t0
        inside = (lane >= lo) & (lane < hi)
        window = slice(128 * t0, 128 * t1)
        qh = jnp.where(inside, q[:, window], 0.0).astype(BF16)
        scores = jnp.where(apart, -1e30, dot_t(qh, k[:, window]))
        att = dot32(softmax(scores), v[:, window])
        att = jnp.where(inside, att, 0.0)
        for t in range(t0, t1):
            part = att[:, 128 * (t - t0) : 128 * (t - t0 + 1)]
            tiles[t] = part if tiles[t] is None else tiles[t] + part
    attended = jnp.concatenate(tiles, 1).astype(BF16)
    waits[5].wait()
    mixed = hidden + mods[5:6] * dot32(attended, wot[...])
    for p in range(5):
        for f in range(8):
            lo = 32 * p + 4 * f
            out[f, p] = mixed[lo : lo + 4].astype(BF16)


def temporal(mods, gain, seg, back, res, wts):
    return pl.pallas_call(
        temporal_kernel,
        out_shape=jax.ShapeDtypeStruct((8, 5, 4, D), BF16),
        in_specs=[VMEM] * 5 + [ANY],
        out_specs=VMEM,
        scratch_shapes=[
            pltpu.VMEM((D, D), BF16),
            pltpu.VMEM((D, D), BF16),
            pltpu.VMEM((D, D), BF16),
            pltpu.VMEM((D, D), BF16),
            pltpu.VMEM((D, D), BF16),
            pltpu.SemaphoreType.DMA((6,)),
        ],
        compiler_params=pltpu.CompilerParams(vmem_limit_bytes=40 * 2**20),
        cost_estimate=pl.CostEstimate(
            flops=1_800_000_000, bytes_accessed=15_000_000, transcendentals=500_000
        ),
    )(mods, gain, seg, back, res, wts)


def in_order(zh, mine, far):
    return jnp.concatenate([jnp.where(zh == 0, mine, far), jnp.where(zh == 0, far, mine)], 0)


def per_device(latent, mod_s, mod_t, gain, wqkv_s, wout_s, wqkv_t, wout_t):
    core = lax.axis_index("core")
    zh = lax.axis_index("zh")
    y = lax.axis_index("y")
    own_zh = lax.rem(zh + core + y // 2, 2)
    place = jnp.stack([y, own_zh]).astype(jnp.int32)
    other = [(0, 1), (1, 0)]
    latent = latent.reshape(4, 40, D)

    stay = lax.dynamic_slice_in_dim(latent, 2 * zh, 2, 0)
    leave = lax.dynamic_slice_in_dim(latent, 2 - 2 * zh, 2, 0)
    moved = lax.ppermute(leave, ("core", "zh"), [(i, 3 - i) for i in range(4)])

    pad = jnp.zeros((36, 2 * CUT - 5 * D), BF16)
    tail = jnp.concatenate([wqkv_t[:, CUT:], wout_s, wout_t, pad], 1)
    half_r = jnp.where(core == 0, wqkv_t[:, :CUT], tail)
    far_r = lax.ppermute(half_r, "zh", other)

    by_pair = wqkv_s.reshape(36, 3, 4, 2, PAIR)
    half_s = lax.dynamic_index_in_dim(by_pair, core, 3, keepdims=False)
    half_s = half_s.transpose(2, 0, 1, 3).reshape(4, 36, 3 * PAIR)
    w_x = lax.all_to_all(half_s, "x", split_axis=0, concat_axis=0, tiled=True)
    moved, w_x, far_r = lax.optimization_barrier((moved, w_x, far_r))
    w_far = lax.ppermute(w_x, "zh", other)
    frames = jnp.concatenate(
        [jnp.where(core == 0, stay, moved), jnp.where(core == 0, moved, stay)], 0
    )
    rows = lax.all_to_all(frames, "y", split_axis=0, concat_axis=0, tiled=True)
    by_home = latent.reshape(4, 8, 5, D).transpose(1, 2, 0, 3)
    rows, by_home = lax.optimization_barrier((rows, by_home))
    copies = norm_copies(mod_s, rows).reshape(4, 160, D)
    copies, w_far = lax.optimization_barrier((copies, w_far))
    weights = lax.all_gather(in_order(zh, half_r, far_r), ("core", "y", "x"), axis=0, tiled=True)

    w_z = jnp.stack([jnp.where(zh == 0, w_x, w_far), jnp.where(zh == 0, w_far, w_x)], 1)
    w_z = w_z.reshape(D // 4, 3 * PAIR)
    w_y = [w_z] + [
        lax.ppermute(w_z, "y", [((i + k) % 4, i) for i in range(4)]) for k in (1, 2, 3)
    ]

    ours = lax.all_to_all(copies, "x", split_axis=0, concat_axis=0, tiled=True).reshape(640, D)
    ours, w_y = lax.optimization_barrier((ours, w_y))
    theirs = lax.ppermute(ours, "core", other)
    by_home, ours = lax.optimization_barrier((by_home, ours))
    home = lax.all_to_all(by_home, ("zl", "core"), split_axis=0, concat_axis=0, tiled=True)
    home = home.transpose(1, 0, 2, 3).reshape(160, D)
    gain_s = jnp.pad(jnp.tile(gain[:2], (1, 2)), ((0, 0), (0, 256 - PAIR)))
    att = spatial(place, gain_s, ours, theirs, *w_y)

    att = att.reshape(2, 4, 4, 4, 2, 5, PAIR).transpose(3, 0, 2, 1, 4, 5, 6)
    att = att.reshape(256, 5, PAIR)
    everyone = ("zl", "zh", "y", "x", "core")
    back = lax.all_to_all(att, everyone, split_axis=0, concat_axis=0, tiled=True)
    back = back.reshape(4, 2, 2, 2, 8, 5, PAIR).transpose(5, 0, 2, 1, 3, 4, 6).reshape(160, D)

    seg = (jnp.arange(D)[:, None] // HDIM == jnp.arange(128)[None]).astype(BF16)
    mods = jnp.concatenate([mod_s, mod_t], 0)
    mixed = temporal(mods, jnp.tile(gain[2:], (1, HEADS)), seg, back, home, weights)
    mixed = lax.all_to_all(mixed, ("zl", "core"), split_axis=0, concat_axis=0, tiled=True)
    return mixed.transpose(2, 0, 1, 3).reshape(4, 1, 40, D)


def solution(mesh):
    fine = Mesh(mesh.devices.reshape(4, 2, 4, 4, 2), ("zl", "core", "y", "x", "zh"))
    frame, row = ("zl", "core"), ("y", "x", "zh")
    in_specs = (
        P(frame, row, None, None),
        P(),
        P(),
        P(),
        P(row, None),
        P(row, None),
        P(row, None),
        P(row, None),
    )
    return jax.shard_map(
        per_device,
        mesh=fine,
        in_specs=in_specs,
        out_specs=P(frame, row, None, None),
        check_vma=False,
    )
```

```python
import jax
import jax.numpy as jnp
from jax import lax
from jax.experimental import pallas as pl
from jax.experimental.pallas import tpu as pltpu
from jax.sharding import Mesh
from jax.sharding import PartitionSpec as P

HEADS = 16
HDIM = 72
D = 1152
PAIR = 2 * HDIM
CUT = 2944
REST = 3 * D - CUT
SCALE = HDIM**-0.5
EXP2 = 1.4426950408889634
F32 = jnp.float32
BF16 = jnp.bfloat16
VMEM = pl.BlockSpec(memory_space=pltpu.VMEM)
SMEM = pl.BlockSpec(memory_space=pltpu.SMEM)
ANY = pl.BlockSpec(memory_space=pl.ANY)


def dot32(a, b):
    return jnp.dot(a, b, preferred_element_type=F32)


def dot_t(a, b):
    return lax.dot_general(a, b, (((1,), (1,)), ((), ())), preferred_element_type=F32)


def modulate(values, shift, scale):
    center = values - jnp.mean(values, -1, keepdims=True)
    variance = jnp.mean(center * center, -1, keepdims=True)
    return (center * lax.rsqrt(variance + 1e-06) * (1.0 + scale) + shift).astype(BF16)


def norm_kernel(mod, rows, out):
    normed = modulate(rows[...].astype(F32), mod[0:1], mod[1:2])
    for copy in range(4):
        out[copy] = normed


def norm_copies(mod, rows):
    return pl.pallas_call(
        norm_kernel,
        out_shape=jax.ShapeDtypeStruct((4, 4, 40, D), BF16),
        in_specs=[VMEM] * 2,
        out_specs=VMEM,
        cost_estimate=pl.CostEstimate(flops=4_000_000, bytes_accessed=2_000_000, transcendentals=0),
    )(mod, rows)


def softmax(scores):
    highest = jnp.max(scores, -1, keepdims=True)
    expo = jnp.exp2((scores - highest) * (SCALE * EXP2))
    return (expo * (1.0 / jnp.sum(expo, -1, keepdims=True))).astype(BF16)


def spatial_kernel(place, gain, tok_ours, tok_theirs, w0, w1, w2, w3, out, wall, q0, q1, k0, v0):
    y, own_zh = place[0], place[1]
    quarter = D // 4
    wall[...] = jnp.zeros_like(wall)
    for k, w in enumerate((w0, w1, w2, w3)):
        rows = pl.ds(pl.multiple_of(lax.rem(y + k, 4) * quarter, quarter), quarter)
        for part in range(2):
            lo = 256 * part
            wall[rows, lo : lo + PAIR] = w[:, PAIR * part : PAIR * (part + 1)]
            head = 2 * PAIR + HDIM * part
            wall[rows, lo + PAIR : lo + PAIR + HDIM] = w[:, head : head + HDIM]
    lane = lax.broadcasted_iota(jnp.int32, (1, 256), 1)
    first = lane < HDIM
    second = (lane >= HDIM) & (lane < PAIR)

    def head_norm(heads, g):
        square = heads * heads
        s0 = jnp.sum(jnp.where(first, square, 0.0), -1, keepdims=True)
        s1 = jnp.sum(jnp.where(second, square, 0.0), -1, keepdims=True)
        r0 = lax.rsqrt(s0 * (1.0 / HDIM) + 1e-06)
        r1 = lax.rsqrt(s1 * (1.0 / HDIM) + 1e-06)
        return heads * jnp.where(first, r0, r1) * g

    for i in range(4):
        at = slice(320 * i, 320 * (i + 1))
        tok = (tok_ours, tok_theirs)[i // 2]
        qkv = dot32(tok[320 * (i % 2) : 320 * (i % 2 + 1)], wall[...])
        q = head_norm(qkv[:, :256], gain[0:1])
        q0[at] = jnp.where(first, q, 0.0).astype(BF16)
        q1[at] = jnp.where(second, q, 0.0).astype(BF16)
        k0[at] = head_norm(qkv[:, 256:512], gain[1:2]).astype(BF16)
        v = jnp.where(first, pltpu.roll(qkv[:, :256], 112, 1), pltpu.roll(qkv[:, 256:], 184, 1))
        v = jnp.where(lane < PAIR, v, jnp.where(lane == PAIR, 1.0, 0.0))
        v0[at] = v.astype(BF16)

    def attend(queries):
        scores = dot_t(queries, k0[...])
        highest = jnp.max(scores, -1, keepdims=True)
        expo = jnp.exp2((scores - highest) * (SCALE * EXP2)).astype(BF16)
        both = dot32(expo, v0[...])
        return both * (1.0 / both[:, PAIR : PAIR + 1])

    for i in range(4):
        at = slice(320 * i, 320 * (i + 1))
        att = jnp.where(first, attend(q0[at]), attend(q1[at]))[:, :PAIR]
        from_zh = own_zh if i < 2 else 1 - own_zh
        for j in range(8):
            out[from_zh * 16 + (i % 2) * 8 + j] = att[40 * j : 40 * (j + 1)].astype(BF16)


def spatial(place, gain, *operands):
    return pl.pallas_call(
        spatial_kernel,
        out_shape=jax.ShapeDtypeStruct((32, 40, PAIR), BF16),
        in_specs=[SMEM] + [VMEM] * 7,
        out_specs=VMEM,
        scratch_shapes=[pltpu.VMEM((D, 512), BF16)] + [pltpu.VMEM((1280, 256), BF16)] * 4,
        compiler_params=pltpu.CompilerParams(vmem_limit_bytes=48 * 2**20),
        cost_estimate=pl.CostEstimate(
            flops=5_000_000_000, bytes_accessed=5_000_000, transcendentals=3_300_000
        ),
    )(place, gain, *operands)


def temporal_kernel(mods, gain, seg, back, res, wts, out, wos, wq, wk, wv, wot, sem):
    parts = [
        (pl.ds(D, D), slice(REST, REST + D), wos),
        (pl.ds(0, D), slice(0, D), wq),
        (pl.ds(0, D), slice(D, 2 * D), wk),
        (pl.ds(0, D), slice(2 * D, CUT), wv.at[:, : CUT - 2 * D]),
        (pl.ds(D, D), slice(0, REST), wv.at[:, CUT - 2 * D :]),
        (pl.ds(D, D), slice(REST + D, REST + 2 * D), wot),
    ]
    waits = [
        pltpu.make_async_copy(wts.at[rows, cols], to, sem.at[i])
        for i, (rows, cols, to) in enumerate(parts)
    ]
    for copy in waits:
        copy.start()
    waits[0].wait()
    hidden = res[...].astype(F32) + mods[2:3] * dot32(back[...], wos[...])
    hidden = hidden.astype(BF16).astype(F32)
    modulated = modulate(hidden, mods[3:4], mods[4:5])

    def head_norm(heads, g):
        square = heads * heads
        high = square.astype(BF16)
        low = (square - high.astype(F32)).astype(BF16)
        mean = (dot32(high, seg[...]) + dot32(low, seg[...])) * (1.0 / HDIM)
        r = lax.rsqrt(mean + 1e-06)
        r_high = r.astype(BF16)
        r_mid = (r - r_high.astype(F32)).astype(BF16)
        r_low = (r - r_high.astype(F32) - r_mid.astype(F32)).astype(BF16)
        wide = dot_t(r_high, seg[...]) + dot_t(r_mid, seg[...]) + dot_t(r_low, seg[...])
        return heads * wide * g

    waits[1].wait()
    q = head_norm(dot32(modulated, wq[...]), gain[0:1])
    waits[2].wait()
    k = head_norm(dot32(modulated, wk[...]), gain[1:2]).astype(BF16)
    waits[3].wait()
    waits[4].wait()
    v = dot32(modulated, wv[...]).astype(BF16)
    row = lax.broadcasted_iota(jnp.int32, (160, 160), 0)
    col = lax.broadcasted_iota(jnp.int32, (160, 160), 1)
    apart = row // 32 != col // 32
    tiles = [None] * (D // 128)
    for h in range(HEADS):
        lo, hi = HDIM * h, HDIM * (h + 1)
        t0, t1 = lo // 128, -(-hi // 128)
        lane = lax.broadcasted_iota(jnp.int32, (1, 128 * (t1 - t0)), 1) + 128 * t0
        inside = (lane >= lo) & (lane < hi)
        window = slice(128 * t0, 128 * t1)
        qh = jnp.where(inside, q[:, window], 0.0).astype(BF16)
        scores = jnp.where(apart, -1e30, dot_t(qh, k[:, window]))
        att = dot32(softmax(scores), v[:, window])
        att = jnp.where(inside, att, 0.0)
        for t in range(t0, t1):
            part = att[:, 128 * (t - t0) : 128 * (t - t0 + 1)]
            tiles[t] = part if tiles[t] is None else tiles[t] + part
    attended = jnp.concatenate(tiles, 1).astype(BF16)
    waits[5].wait()
    mixed = hidden + mods[5:6] * dot32(attended, wot[...])
    for p in range(5):
        for f in range(8):
            lo = 32 * p + 4 * f
            out[f, p] = mixed[lo : lo + 4].astype(BF16)


def temporal(mods, gain, seg, back, res, wts):
    return pl.pallas_call(
        temporal_kernel,
        out_shape=jax.ShapeDtypeStruct((8, 5, 4, D), BF16),
        in_specs=[VMEM] * 5 + [ANY],
        out_specs=VMEM,
        scratch_shapes=[
            pltpu.VMEM((D, D), BF16),
            pltpu.VMEM((D, D), BF16),
            pltpu.VMEM((D, D), BF16),
            pltpu.VMEM((D, D), BF16),
            pltpu.VMEM((D, D), BF16),
            pltpu.SemaphoreType.DMA((6,)),
        ],
        compiler_params=pltpu.CompilerParams(vmem_limit_bytes=40 * 2**20),
        cost_estimate=pl.CostEstimate(
            flops=1_800_000_000, bytes_accessed=15_000_000, transcendentals=500_000
        ),
    )(mods, gain, seg, back, res, wts)


def in_order(zh, mine, far):
    return jnp.concatenate([jnp.where(zh == 0, mine, far), jnp.where(zh == 0, far, mine)], 0)


def per_device(latent, mod_s, mod_t, gain, wqkv_s, wout_s, wqkv_t, wout_t):
    core = lax.axis_index("core")
    zh = lax.axis_index("zh")
    y = lax.axis_index("y")
    own_zh = lax.rem(zh + core + y // 2, 2)
    place = jnp.stack([y, own_zh]).astype(jnp.int32)
    other = [(0, 1), (1, 0)]
    latent = latent.reshape(4, 40, D)

    stay = lax.dynamic_slice_in_dim(latent, 2 * zh, 2, 0)
    leave = lax.dynamic_slice_in_dim(latent, 2 - 2 * zh, 2, 0)
    moved = lax.ppermute(leave, ("core", "zh"), [(i, 3 - i) for i in range(4)])

    pad = jnp.zeros((36, 2 * CUT - 5 * D), BF16)
    tail = jnp.concatenate([wqkv_t[:, CUT:], wout_s, wout_t, pad], 1)
    half_r = jnp.where(core == 0, wqkv_t[:, :CUT], tail)
    far_r = lax.ppermute(half_r, "zh", other)

    by_pair = wqkv_s.reshape(36, 3, 4, 2, PAIR)
    half_s = lax.dynamic_index_in_dim(by_pair, core, 3, keepdims=False)
    half_s = half_s.transpose(2, 0, 1, 3).reshape(4, 36, 3 * PAIR)
    w_x = lax.all_to_all(half_s, "x", split_axis=0, concat_axis=0, tiled=True)
    moved, w_x, far_r = lax.optimization_barrier((moved, w_x, far_r))
    w_far = lax.ppermute(w_x, "zh", other)
    frames = jnp.concatenate(
        [jnp.where(core == 0, stay, moved), jnp.where(core == 0, moved, stay)], 0
    )
    rows = lax.all_to_all(frames, "y", split_axis=0, concat_axis=0, tiled=True)
    by_home = latent.reshape(4, 8, 5, D).transpose(1, 2, 0, 3)
    rows, by_home = lax.optimization_barrier((rows, by_home))
    copies = norm_copies(mod_s, rows).reshape(4, 160, D)
    copies, w_far = lax.optimization_barrier((copies, w_far))
    weights = lax.all_gather(in_order(zh, half_r, far_r), ("core", "y", "x"), axis=0, tiled=True)

    w_z = jnp.stack([jnp.where(zh == 0, w_x, w_far), jnp.where(zh == 0, w_far, w_x)], 1)
    w_z = w_z.reshape(D // 4, 3 * PAIR)
    w_y = [w_z] + [
        lax.ppermute(w_z, "y", [((i + k) % 4, i) for i in range(4)]) for k in (1, 2, 3)
    ]

    ours = lax.all_to_all(copies, "x", split_axis=0, concat_axis=0, tiled=True).reshape(640, D)
    ours, w_y = lax.optimization_barrier((ours, w_y))
    theirs = lax.ppermute(ours, "core", other)
    by_home, ours = lax.optimization_barrier((by_home, ours))
    home = lax.all_to_all(by_home, ("zl", "core"), split_axis=0, concat_axis=0, tiled=True)
    home = home.transpose(1, 0, 2, 3).reshape(160, D)
    gain_s = jnp.pad(jnp.tile(gain[:2], (1, 2)), ((0, 0), (0, 256 - PAIR)))
    att = spatial(place, gain_s, ours, theirs, *w_y)

    att = att.reshape(2, 4, 4, 4, 2, 5, PAIR).transpose(3, 0, 2, 1, 4, 5, 6)
    att = att.reshape(256, 5, PAIR)
    everyone = ("zl", "zh", "y", "x", "core")
    back = lax.all_to_all(att, everyone, split_axis=0, concat_axis=0, tiled=True)
    back = back.reshape(4, 2, 2, 2, 8, 5, PAIR).transpose(5, 0, 2, 1, 3, 4, 6).reshape(160, D)

    seg = (jnp.arange(D)[:, None] // HDIM == jnp.arange(128)[None]).astype(BF16)
    mods = jnp.concatenate([mod_s, mod_t], 0)
    mixed = temporal(mods, jnp.tile(gain[2:], (1, HEADS)), seg, back, home, weights)
    mixed = lax.all_to_all(mixed, ("zl", "core"), split_axis=0, concat_axis=0, tiled=True)
    return mixed.transpose(2, 0, 1, 3).reshape(4, 1, 40, D)


def solution(mesh):
    fine = Mesh(mesh.devices.reshape(4, 2, 4, 4, 2), ("zl", "core", "y", "x", "zh"))
    frame, row = ("zl", "core"), ("y", "x", "zh")
    in_specs = (
        P(frame, row, None, None),
        P(),
        P(),
        P(),
        P(row, None),
        P(row, None),
        P(row, None),
        P(row, None),
    )
    return jax.shard_map(
        per_device,
        mesh=fine,
        in_specs=in_specs,
        out_specs=P(frame, row, None, None),
        check_vma=False,
    )
```
